32 devices in a mesh: groups: 2 (over x), pairs: 16 (over z, y, core).
Axes of the slice: x: 2, y: 2, z: 4, core: 2. Of those that a mesh axis runs over, the one named last changes fastest.
Arguments:
- amplitudes: bfloat16 [2048, 128, 128], P(('groups', 'pairs')), parts along dimension 0, may hold values from -6 to 6
- pair_tiles: int32 [2048, 4], P('groups'), parts along dimension 0, may hold values from 0 to 31, as said below
- fit_vv: bfloat16 [24, 128, 16, 128], P('groups', 'pairs'), parts along dimension 0, as said below
- fit_ov: bfloat16 [64, 12, 16, 128], P(('groups', 'pairs')), parts along dimension 0, may hold values from -0.890625 to 0.890625
Outputs:
- residual: bfloat16 [2048, 128, 128], P(('groups', 'pairs')), parts along dimension 0
The draws below stay inside these ranges and needn't reach their ends.
There are 2 independent parts, one for each index of `groups`. The reference program is written for one: setup_inputs(seed, part) draws one part's arguments, and reference() takes and returns one part's arrays. A program takes and returns all parts, laid end to end along the dimension named above; each array names one. Nothing has to cross between parts.
Inputs may be any that keep to these rules, and one draw needn't show every extreme that they name: `pair_tiles`: row r of the device s = r // 64 has k = s * 2 + r % 2. Column 1 is j, column 2 is A, column 3 is B; A and B are below 12. Among the rows of one device at most 4 have the same j // 2, and on every device some value of j // 2 is taken by exactly 4 rows. fit_vv[A, x, q, y] = fit_vv[A, y, q, x].
All inputs are finite; a program needn't handle non-finite values.
Results may differ from the reference program's by a relative error of at most 0.0049.
Values may be sent and summed in bfloat16 or wider, within the bound.
A program may use at most 128 MiB of HBM per device.

```python
import jax
import jax.numpy as jnp
from jax import lax

VT = 128
NVT = 12
NQ = 16
OCC_DEV = 2
PPD = 64
CAP = 4
NOCC = 32
NPAIR = 1024
N_PAIRS = 16


def draw_pair_tiles(key, part):
    key = jax.random.fold_in(key, 11)
    hot_key, dev_key = jax.random.split(key)
    hotness = jax.random.randint(hot_key, (N_PAIRS,), 0, 3)
    entries = jnp.arange(N_PAIRS * CAP, dtype=jnp.int32)
    owners_of = entries // CAP

    def one_device(sub, device):
        k1, k2, k3, k4, k5, k6 = jax.random.split(sub, 6)
        favored = jax.random.randint(k1, (), 0, N_PAIRS)
        noise = jax.random.randint(k2, (N_PAIRS * CAP,), 0, 4096)
        score = hotness[owners_of] * 4096 + noise + 4 * 4096 * (owners_of == favored).astype(jnp.int32)
        score = score * (N_PAIRS * CAP) + entries
        top_scores, picked = jax.lax.top_k(score, PPD)
        order = jax.random.permutation(k3, PPD)
        dest = owners_of[picked][order]
        occ_j = dest * OCC_DEV + jax.random.randint(k4, (PPD,), 0, OCC_DEV)
        occ_k = device * OCC_DEV + jnp.arange(PPD, dtype=jnp.int32) % OCC_DEV
        tile_a = jax.random.randint(k5, (PPD,), 0, NVT)
        tile_b = jax.random.randint(k6, (PPD,), 0, NVT)
        return jnp.stack([occ_k, occ_j, tile_a, tile_b], axis=1)
    subs = jax.random.split(dev_key, N_PAIRS)
    rows = jax.vmap(one_device)(subs, jnp.arange(N_PAIRS, dtype=jnp.int32))
    return rows.reshape(N_PAIRS * PPD, 4).astype(jnp.int32)


def draw_fit_vv(key, part):
    key = jax.random.fold_in(key, 23)
    scale = (NQ * VT * VT) ** (-0.25)
    raw = jax.random.normal(key, (NVT, VT, NQ, VT), jnp.float32)
    both = (raw + jnp.transpose(raw, (0, 3, 2, 1))) * 0.70710678
    return (both * scale).astype(jnp.bfloat16)


def block_scale(own_key, dims, cuts, smallest, largest):
    def one(axis_at, parts):
        steps = jax.random.uniform(jax.random.fold_in(jax.random.fold_in(own_key, 6), axis_at), (parts,), jnp.float32, smallest / len(cuts), largest / len(cuts))
        return jnp.repeat(jnp.exp(steps), dims[axis_at] // parts).reshape((-1,) + (1,) * (len(dims) - axis_at - 1))

    loudness = one(*cuts[0])
    for cut in cuts[1:]:
        loudness = loudness * one(*cut)
    return loudness


def normal_values(key, extent, scale, limit, shards=(), kind=jnp.bfloat16):
    loudness = block_scale(key, extent, shards, -0.22, 0.18) if shards else 1.0
    result = jax.random.normal(key, extent, jnp.float32) * scale * loudness
    return jnp.minimum(jnp.maximum(result, -limit), limit).astype(kind)


def setup_inputs(seed: int = 0, part: int = 0) -> dict:
    key_of = jax.random.split(jax.random.key(seed), 5)
    part_keys = jax.random.split(jax.random.fold_in(key_of[4], part), 5)
    return {
        "amplitudes": normal_values(part_keys[0], (NPAIR, VT, VT), 1.0, 6.0, ((0, 16),)),
        "pair_tiles": draw_pair_tiles(jax.random.fold_in(jax.random.fold_in(key_of[4], part), 71), part),
        "fit_vv": draw_fit_vv(jax.random.fold_in(jax.random.fold_in(key_of[4], part), 71), part),
        "fit_ov": normal_values(part_keys[3], (NOCC, NVT, NQ, VT), ((NQ * VT) ** -0.25), 0.890625, ((0, 16),)),
    }


def ladder_tile(args, fit_vv):
    tile, left_id, right_id = args
    right = fit_vv[right_id].astype(jnp.float32)
    left = fit_vv[left_id].astype(jnp.float32)
    inner = jnp.einsum('cd,dqb->cqb', tile.astype(jnp.float32), right).astype(jnp.bfloat16)
    return jnp.einsum('aqc,cqb->ab', left, inner.astype(jnp.float32))


def reference(amplitudes, pair_tiles, fit_vv, fit_ov):
    occ_k = pair_tiles[:, 0]
    occ_j = pair_tiles[:, 1]
    tile_a = pair_tiles[:, 2]
    tile_b = pair_tiles[:, 3]
    ladder = lax.map(lambda args: ladder_tile(args, fit_vv), (amplitudes, tile_a, tile_b))
    fit_rows = fit_ov[occ_k, tile_a].astype(jnp.float32)
    partial_value = jnp.einsum('pqc,pcb->pqb', fit_rows, amplitudes.astype(jnp.float32), precision=lax.Precision.HIGHEST)
    column = (occ_j * NVT + tile_b).astype(jnp.int32)
    totals = jax.ops.segment_sum(partial_value, column, num_segments=NOCC * NVT)
    chosen = totals[column]
    cycle = jnp.einsum('pqa,pqb->pab', fit_rows, chosen, precision=lax.Precision.HIGHEST).astype(jnp.bfloat16)
    cycle = lax.optimization_barrier(cycle)
    return (ladder + cycle.astype(jnp.float32)).astype(jnp.bfloat16)
```

```python
import functools

import jax
import jax.numpy as jnp
from jax import lax
from jax.experimental import pallas as pl
from jax.experimental.pallas import tpu as pltpu
from jax.sharding import PartitionSpec as P

F32 = jnp.float32
BF16 = jnp.bfloat16


def grid_of(n):
    ny = 2 if n == 16 else 1
    return n // (2 * ny), ny


def comm_kernel(
    n, cap, fit_count,
    perm_ref, row_ref, vv_ref, amp_ref, fit_ref, code_col_ref, code_row_ref,
    v_ref, chosen_ref,
    gbuf, part, inbuf, back,
    send_sem, recv_sem, go_send, go_recv, ret_send, ret_recv,
):
    nz, ny = grid_of(n)
    me = lax.axis_index("pairs")
    z, y, c = me // (2 * ny), (me // 2) % ny, me % 2
    vtiles, rows_dev = vv_ref.shape[0], vv_ref.shape[1]
    block = cap * fit_count

    def index(zz, yy, cc):
        return (zz * ny + yy) * 2 + cc

    barrier = pltpu.get_barrier_semaphore()
    for off in range(1, n):
        pl.semaphore_signal(barrier, inc=1, device_id={"pairs": (me + off) % n},
                            device_id_type=pl.DeviceIdType.MESH)
    pl.semaphore_wait(barrier, n - 1)

    def remote(src, dst, ssem, rsem, dev):
        return pltpu.make_async_remote_copy(
            src_ref=src, dst_ref=dst, send_sem=ssem, recv_sem=rsem,
            device_id={"pairs": dev}, device_id_type=pl.DeviceIdType.MESH)

    started = []

    def send(src, shard, dev, cond):
        k = len(started)
        cp = remote(src, gbuf.at[shard], send_sem.at[k], recv_sem.at[shard], dev)
        started.append((cp, cond))
        if cond is None:
            cp.start()
        else:
            pl.when(cond)(cp.start)

    def arrived(shard, cond=None):
        cp = remote(gbuf.at[shard], gbuf.at[shard], send_sem.at[0], recv_sem.at[shard], me)
        if cond is None:
            cp.wait_recv()
        else:
            pl.when(cond)(cp.wait_recv)

    up_ok, down_ok = z + 1 < nz, z >= 1
    up, down = jnp.minimum(z + 1, nz - 1), jnp.maximum(z - 1, 0)
    send(vv_ref, me, index(up, y, c), up_ok)
    send(vv_ref, me, index(down, y, c), down_ok)
    if ny == 2:
        send(vv_ref, me, index(z, 1 - y, c), None)
    send(vv_ref, me, index(z, y, 1 - c), None)

    def one_partial(s, carry):
        p = perm_ref[s]
        val = jnp.dot(fit_ref[row_ref[s]], amp_ref[p], preferred_element_type=F32)
        part[pl.ds(pl.multiple_of(s * fit_count, fit_count), fit_count), :] = val.astype(BF16)
        return carry

    lax.fori_loop(0, n * cap, one_partial, 0, unroll=4)

    def slab(ref, i):
        return ref.at[pl.ds(pl.multiple_of(i * block, block), block)]

    go = []
    for off in range(1, n):
        dev = (me + off) % n
        cp = remote(slab(part, dev), slab(inbuf, me), go_send.at[off], go_recv.at[off], dev)
        cp.start()
        go.append(cp)
    here = pl.ds(pl.multiple_of(me * block, block), block)
    inbuf[here, :] = part[here, :]

    def z_step(k):
        for zz, okay, nxt, nxt_ok in ((z - k, z >= k, up, up_ok), (z + k, z + k < nz, down, down_ok)):
            zs = jnp.clip(zz, 0, nz - 1)
            shard = index(zs, y, c)
            arrived(shard, okay)
            src = gbuf.at[shard]
            send(src, shard, index(nxt, y, c), jnp.logical_and(okay, nxt_ok))
            if ny == 2:
                send(src, shard, index(z, 1 - y, c), okay)
            send(src, shard, index(z, y, 1 - c), okay)

    z_step(1)

    for cp in go:
        cp.wait_recv()
    total_rows = n * block
    mt = 256
    code_row = code_row_ref[...]
    values = inbuf[...]

    def totals(i, carry):
        r = pl.ds(pl.multiple_of(i * mt, mt), mt)
        same = jnp.where(code_col_ref[r, :] == code_row, 1.0, 0.0).astype(BF16)
        back[r, :] = jnp.dot(same, values, preferred_element_type=F32).astype(BF16)
        return carry

    lax.fori_loop(0, total_rows // mt, totals, 0)
    ret = []
    for off in range(1, n):
        dev = (me + off) % n
        cp = remote(slab(back, dev), slab(chosen_ref, me), ret_send.at[off], ret_recv.at[off], dev)
        cp.start()
        ret.append(cp)
    chosen_ref[here, :] = back[here, :]

    for k in range(2, nz):
        z_step(k)

    def relayout(lo, hi, m):
        if rows_dev != 8:
            return

        def one(i, carry):
            a0 = lo[i].astype(F32)
            a1 = hi[i].astype(F32)
            rows = pl.ds(pl.multiple_of(m * 16, 16), 16)
            for h in range(rows_dev):
                for e in range(2):
                    both = jnp.concatenate(
                        [a0[h, 8 * e:8 * e + 8], a1[h, 8 * e:8 * e + 8]], axis=0)
                    v_ref[i, 2 * h + e, rows, :] = both.astype(BF16)
            return carry

        lax.fori_loop(0, vtiles, one, 0)

    def chip(zz, yy):
        base = index(zz, yy, 0)
        relayout(gbuf.at[base], gbuf.at[base + 1], base // 2)

    gbuf[me] = vv_ref[...]
    for k in range(nz):
        zz = (z + k) % nz
        arrived(index(zz, y, 1 - c))
        chip(zz, y)
    if ny == 2:
        order = [(z, None)]
        for k in range(1, nz):
            order += [(z - k, z >= k), (z + k, z + k < nz)]
        for zz, cond in order:
            shard = index(jnp.clip(zz, 0, nz - 1), 1 - y, c)
            arrived(shard, cond)
            send(gbuf.at[shard], shard, index(z, y, 1 - c), cond)
        for zz, cond in order:
            zc = jnp.clip(zz, 0, nz - 1)

            def finish(zc=zc):
                arrived(index(zc, 1 - y, 1 - c))
                chip(zc, 1 - y)

            if cond is None:
                finish()
            else:
                pl.when(cond)(finish)
    if rows_dev != 8:
        for i in range(n):
            v_ref[:, i * rows_dev:(i + 1) * rows_dev] = gbuf[i]
    for cp in ret:
        cp.wait_recv()
    for cp in go + ret:
        cp.wait_send()
    for cp, cond in started:
        if cond is None:
            cp.wait_send()
        else:
            pl.when(cond)(cp.wait_send)


def ladder_kernel(a_ids, b_ids, fit_ids, slots, v_ref, amp_ref, fit_ref, chosen_ref, out_ref):
    tiles = amp_ref.shape[0]
    q_count = v_ref.shape[1]
    width = v_ref.shape[2]

    def one(p, carry):
        left, right = v_ref[a_ids[p]], v_ref[b_ids[p]]
        wide = jnp.concatenate([right[q] for q in range(q_count)], axis=1)
        inner = jnp.dot(amp_ref[p], wide, preferred_element_type=F32).astype(BF16)
        tall = jnp.concatenate(
            [inner[:, q * width:(q + 1) * width] for q in range(q_count)], axis=0)
        acc = jnp.dot(
            jnp.concatenate([left[q] for q in range(q_count)], axis=1), tall,
            preferred_element_type=F32)
        cyc = lax.dot_general(
            fit_ref[fit_ids[p]], chosen_ref[slots[p]], (((0,), (0,)), ((), ())),
            preferred_element_type=F32).astype(BF16)
        out_ref[p] = (acc + cyc.astype(F32)).astype(BF16)
        return carry

    lax.fori_loop(0, tiles, one, 0, unroll=2)


def body(amplitudes, pair_tiles, fit_vv, fit_ov):
    tiles_dev, width = amplitudes.shape[0], amplitudes.shape[1]
    n = lax.axis_size("pairs")
    cap = max(2, tiles_dev // n)
    slots_n = n * cap
    occ_dev, vtiles, fit_count = fit_ov.shape[0], fit_ov.shape[1], fit_ov.shape[2]
    rows_dev = fit_vv.shape[1]
    here = lax.axis_index("pairs")
    mine = lax.dynamic_slice_in_dim(pair_tiles, here * tiles_dev, tiles_dev, 0)
    tile_a, tile_b = mine[:, 2], mine[:, 3]
    dest = mine[:, 1] // occ_dev
    fit_ids = mine[:, 0] % occ_dev * vtiles + tile_a
    steps = jnp.arange(tiles_dev, dtype=jnp.int32)
    earlier = steps[None, :] < steps[:, None]
    rank = jnp.sum(((dest[:, None] == dest[None, :]) & earlier).astype(jnp.int32), axis=1)
    slot = dest * cap + rank
    hit = (slot[None, :] == jnp.arange(slots_n, dtype=jnp.int32)[:, None]).astype(jnp.int32)
    perm = jnp.sum(hit * steps[None, :], axis=1)
    slot_fit = jnp.sum(hit * fit_ids[None, :], axis=1)

    every = pair_tiles.reshape(n, tiles_dev, 4)
    to_here = every[:, :, 1] // occ_dev == here
    order_in = jnp.sum((to_here[:, None, :] & earlier[None]).astype(jnp.int32), axis=2)
    column = every[:, :, 1] % occ_dev * vtiles + every[:, :, 3]
    picked = to_here[:, :, None] & (order_in[:, :, None] == jnp.arange(cap, dtype=jnp.int32))
    code = jnp.sum(jnp.where(picked, column[:, :, None] + 1, 0), axis=1) - 1
    code = code.reshape(slots_n, 1) * fit_count + jnp.arange(fit_count, dtype=jnp.int32)[None, :]
    code = code.reshape(slots_n * fit_count)

    own = fit_vv
    if rows_dev == 8:
        own = jnp.transpose(fit_vv, (0, 2, 1, 3)).reshape(vtiles, rows_dev, 16, width)
    fits = fit_ov.reshape(occ_dev * vtiles, fit_count, width)

    vmem = pl.BlockSpec(memory_space=pltpu.VMEM)
    smem = pl.BlockSpec(memory_space=pltpu.SMEM)
    nz, ny = grid_of(n)
    sends = 4 + 6 * (nz - 1) + 2 * nz
    dma = pltpu.SemaphoreType.DMA
    v_shape = (vtiles, fit_count, width, width) if rows_dev == 8 else (vtiles, width, fit_count, width)
    flat = (slots_n * fit_count, width)
    whole, chosen = pl.pallas_call(
        functools.partial(comm_kernel, n, cap, fit_count),
        out_shape=(jax.ShapeDtypeStruct(v_shape, BF16), jax.ShapeDtypeStruct(flat, BF16)),
        in_specs=[smem, smem, vmem, vmem, vmem, vmem, vmem],
        out_specs=(vmem, vmem),
        scratch_shapes=[
            pltpu.VMEM((n, vtiles, rows_dev, 16, width), BF16),
            pltpu.VMEM(flat, BF16),
            pltpu.VMEM(flat, BF16),
            pltpu.VMEM(flat, BF16),
            dma((sends,)),
            dma((n,)),
            dma((n,)),
            dma((n,)),
            dma((n,)),
            dma((n,)),
        ],
        compiler_params=pltpu.CompilerParams(
            collective_id=0, has_side_effects=True, vmem_limit_bytes=48 * 2**20),
        name="gather_and_totals",
    )(perm, slot_fit, own, amplitudes, fits, code[:, None], code[None, :])
    if rows_dev != 8:
        whole = jnp.transpose(whole, (0, 2, 1, 3))
    chosen = chosen.reshape(slots_n, fit_count, width)
    flops = 4 * tiles_dev * fit_count * width**3
    return pl.pallas_call(
        ladder_kernel,
        out_shape=jax.ShapeDtypeStruct(amplitudes.shape, BF16),
        in_specs=[smem, smem, smem, smem, vmem, vmem, vmem, vmem],
        out_specs=vmem,
        compiler_params=pltpu.CompilerParams(vmem_limit_bytes=48 * 2**20),
        cost_estimate=pl.CostEstimate(flops=flops, bytes_accessed=12 * 2**20, transcendentals=0),
        name="ladder",
    )(tile_a, tile_b, fit_ids, slot, whole, amplitudes, fits, chosen)


def solution(mesh):
    in_specs = (
        P(("groups", "pairs"), None, None),
        P("groups", None),
        P("groups", "pairs", None, None),
        P(("groups", "pairs"), None, None, None),
    )
    out_specs = P(("groups", "pairs"), None, None)
    return jax.shard_map(body, mesh=mesh, in_specs=in_specs, out_specs=out_specs, check_vma=False)
```

```python
import functools

import jax
import jax.numpy as jnp
from jax import lax
from jax.experimental import pallas as pl
from jax.experimental.pallas import tpu as pltpu
from jax.sharding import PartitionSpec as P

F32 = jnp.float32
BF16 = jnp.bfloat16


CHUNKS = 4


def grid_of(n):
    ny = 2 if n == 16 else 1
    return n // (2 * ny), ny


def comm_kernel(
    n, cap, fit_count,
    perm_ref, row_ref, vv_ref, amp_ref, fit_ref, code_col_ref, code_row_ref,
    v_ref, chosen_ref,
    gbuf, part, inbuf, back,
    send_sem, recv_sem, go_send, go_recv, ret_send, ret_recv,
):
    nz, ny = grid_of(n)
    me = lax.axis_index("pairs")
    z, y, c = me // (2 * ny), (me // 2) % ny, me % 2
    vtiles, rows_dev = vv_ref.shape[0], vv_ref.shape[1]
    block = cap * fit_count

    def index(zz, yy, cc):
        return (zz * ny + yy) * 2 + cc

    barrier = pltpu.get_barrier_semaphore()
    for off in range(1, n):
        pl.semaphore_signal(barrier, inc=1, device_id={"pairs": (me + off) % n},
                            device_id_type=pl.DeviceIdType.MESH)
    pl.semaphore_wait(barrier, n - 1)

    def remote(src, dst, ssem, rsem, dev):
        return pltpu.make_async_remote_copy(
            src_ref=src, dst_ref=dst, send_sem=ssem, recv_sem=rsem,
            device_id={"pairs": dev}, device_id_type=pl.DeviceIdType.MESH)

    started = []

    per = vtiles // CHUNKS

    def send(src, shard, h, dev, cond):
        k = len(started)
        part_of = pl.ds(h * per, per)
        cp = remote(src.at[part_of], gbuf.at[shard, part_of], send_sem.at[k],
                    recv_sem.at[shard * CHUNKS + h], dev)
        started.append((cp, cond))
        if cond is None:
            cp.start()
        else:
            pl.when(cond)(cp.start)

    def arrived(shard, h, cond=None):
        ref = gbuf.at[shard, pl.ds(h * per, per)]
        cp = remote(ref, ref, send_sem.at[0], recv_sem.at[shard * CHUNKS + h], me)
        if cond is None:
            cp.wait_recv()
        else:
            pl.when(cond)(cp.wait_recv)

    up_ok, down_ok = z + 1 < nz, z >= 1
    up, down = jnp.minimum(z + 1, nz - 1), jnp.maximum(z - 1, 0)
    for h in range(CHUNKS):
        send(vv_ref, me, h, index(up, y, c), up_ok)
        send(vv_ref, me, h, index(down, y, c), down_ok)
        if ny == 2:
            send(vv_ref, me, h, index(z, 1 - y, c), None)
        send(vv_ref, me, h, index(z, y, 1 - c), None)

    def one_partial(s, carry):
        p = perm_ref[s]
        val = jnp.dot(fit_ref[row_ref[s]], amp_ref[p], preferred_element_type=F32)
        part[pl.ds(pl.multiple_of(s * fit_count, fit_count), fit_count), :] = val.astype(BF16)
        return carry

    lax.fori_loop(0, n * cap, one_partial, 0, unroll=4)

    def slab(ref, i):
        return ref.at[pl.ds(pl.multiple_of(i * block, block), block)]

    go = []
    for off in range(1, n):
        dev = (me + off) % n
        cp = remote(slab(part, dev), slab(inbuf, me), go_send.at[off], go_recv.at[off], dev)
        cp.start()
        go.append(cp)
    here = pl.ds(pl.multiple_of(me * block, block), block)
    inbuf[here, :] = part[here, :]

    def z_step(k):
        for h in range(CHUNKS):
            for zz, okay, nxt, nxt_ok in ((z - k, z >= k, up, up_ok), (z + k, z + k < nz, down, down_ok)):
                zs = jnp.clip(zz, 0, nz - 1)
                shard = index(zs, y, c)
                arrived(shard, h, okay)
                src = gbuf.at[shard]
                send(src, shard, h, index(nxt, y, c), jnp.logical_and(okay, nxt_ok))
                if ny == 2:
                    send(src, shard, h, index(z, 1 - y, c), okay)
                send(src, shard, h, index(z, y, 1 - c), okay)

    for k in range(1, nz):
        z_step(k)

    for cp in go:
        cp.wait_recv()
    total_rows = n * block
    mt = 256
    code_row = code_row_ref[...]
    values = inbuf[...]

    def totals(i, carry):
        r = pl.ds(pl.multiple_of(i * mt, mt), mt)
        same = jnp.where(code_col_ref[r, :] == code_row, 1.0, 0.0).astype(BF16)
        back[r, :] = jnp.dot(same, values, preferred_element_type=F32).astype(BF16)
        return carry

    lax.fori_loop(0, total_rows // mt, totals, 0)
    ret = []
    for off in range(1, n):
        dev = (me + off) % n
        cp = remote(slab(back, dev), slab(chosen_ref, me), ret_send.at[off], ret_recv.at[off], dev)
        cp.start()
        ret.append(cp)
    chosen_ref[here, :] = back[here, :]

    def relayout(lo, hi, m):
        if rows_dev != 8:
            return

        def one(i, carry):
            a0 = lo[i].astype(F32)
            a1 = hi[i].astype(F32)
            rows = pl.ds(pl.multiple_of(m * 16, 16), 16)
            for h in range(rows_dev):
                for e in range(2):
                    both = jnp.concatenate(
                        [a0[h, 8 * e:8 * e + 8], a1[h, 8 * e:8 * e + 8]], axis=0)
                    v_ref[i, 2 * h + e, rows, :] = both.astype(BF16)
            return carry

        lax.fori_loop(0, vtiles, one, 0)

    def chip(zz, yy):
        base = index(zz, yy, 0)
        relayout(gbuf.at[base], gbuf.at[base + 1], base // 2)

    gbuf[me] = vv_ref[...]
    for k in range(nz):
        zz = (z + k) % nz
        for h in range(CHUNKS):
            arrived(index(zz, y, 1 - c), h)
        chip(zz, y)
    if ny == 2:
        order = [(z, None)]
        for k in range(1, nz):
            order += [(z - k, z >= k), (z + k, z + k < nz)]
        for zz, cond in order:
            shard = index(jnp.clip(zz, 0, nz - 1), 1 - y, c)
            for h in range(CHUNKS):
                arrived(shard, h, cond)
                send(gbuf.at[shard], shard, h, index(z, y, 1 - c), cond)
        for zz, cond in order:
            zc = jnp.clip(zz, 0, nz - 1)

            def finish(zc=zc):
                for h in range(CHUNKS):
                    arrived(index(zc, 1 - y, 1 - c), h)
                chip(zc, 1 - y)

            if cond is None:
                finish()
            else:
                pl.when(cond)(finish)
    if rows_dev != 8:
        for i in range(n):
            v_ref[:, i * rows_dev:(i + 1) * rows_dev] = gbuf[i]
    for cp in ret:
        cp.wait_recv()
    for cp in go + ret:
        cp.wait_send()
    for cp, cond in started:
        if cond is None:
            cp.wait_send()
        else:
            pl.when(cond)(cp.wait_send)


def ladder_kernel(a_ids, b_ids, fit_ids, slots, v_ref, amp_ref, fit_ref, chosen_ref, out_ref):
    tiles = amp_ref.shape[0]
    q_count = v_ref.shape[1]
    width = v_ref.shape[2]

    def one(p, carry):
        left, right = v_ref[a_ids[p]], v_ref[b_ids[p]]
        wide = jnp.concatenate([right[q] for q in range(q_count)], axis=1)
        inner = jnp.dot(amp_ref[p], wide, preferred_element_type=F32).astype(BF16)
        tall = jnp.concatenate(
            [inner[:, q * width:(q + 1) * width] for q in range(q_count)], axis=0)
        acc = jnp.dot(
            jnp.concatenate([left[q] for q in range(q_count)], axis=1), tall,
            preferred_element_type=F32)
        cyc = lax.dot_general(
            fit_ref[fit_ids[p]], chosen_ref[slots[p]], (((0,), (0,)), ((), ())),
            preferred_element_type=F32).astype(BF16)
        out_ref[p] = (acc + cyc.astype(F32)).astype(BF16)
        return carry

    lax.fori_loop(0, tiles, one, 0, unroll=2)


def body(amplitudes, pair_tiles, fit_vv, fit_ov):
    tiles_dev, width = amplitudes.shape[0], amplitudes.shape[1]
    n = lax.axis_size("pairs")
    cap = max(2, tiles_dev // n)
    slots_n = n * cap
    occ_dev, vtiles, fit_count = fit_ov.shape[0], fit_ov.shape[1], fit_ov.shape[2]
    rows_dev = fit_vv.shape[1]
    here = lax.axis_index("pairs")
    mine = lax.dynamic_slice_in_dim(pair_tiles, here * tiles_dev, tiles_dev, 0)
    tile_a, tile_b = mine[:, 2], mine[:, 3]
    dest = mine[:, 1] // occ_dev
    fit_ids = mine[:, 0] % occ_dev * vtiles + tile_a
    steps = jnp.arange(tiles_dev, dtype=jnp.int32)
    earlier = steps[None, :] < steps[:, None]
    rank = jnp.sum(((dest[:, None] == dest[None, :]) & earlier).astype(jnp.int32), axis=1)
    slot = dest * cap + rank
    hit = (slot[None, :] == jnp.arange(slots_n, dtype=jnp.int32)[:, None]).astype(jnp.int32)
    perm = jnp.sum(hit * steps[None, :], axis=1)
    slot_fit = jnp.sum(hit * fit_ids[None, :], axis=1)

    every = pair_tiles.reshape(n, tiles_dev, 4)
    to_here = every[:, :, 1] // occ_dev == here
    order_in = jnp.sum((to_here[:, None, :] & earlier[None]).astype(jnp.int32), axis=2)
    column = every[:, :, 1] % occ_dev * vtiles + every[:, :, 3]
    picked = to_here[:, :, None] & (order_in[:, :, None] == jnp.arange(cap, dtype=jnp.int32))
    code = jnp.sum(jnp.where(picked, column[:, :, None] + 1, 0), axis=1) - 1
    code = code.reshape(slots_n, 1) * fit_count + jnp.arange(fit_count, dtype=jnp.int32)[None, :]
    code = code.reshape(slots_n * fit_count)

    own = fit_vv
    if rows_dev == 8:
        own = jnp.transpose(fit_vv, (0, 2, 1, 3)).reshape(vtiles, rows_dev, 16, width)
    fits = fit_ov.reshape(occ_dev * vtiles, fit_count, width)

    vmem = pl.BlockSpec(memory_space=pltpu.VMEM)
    smem = pl.BlockSpec(memory_space=pltpu.SMEM)
    nz, ny = grid_of(n)
    sends = 4 + 6 * (nz - 1) + 2 * nz
    dma = pltpu.SemaphoreType.DMA
    v_shape = (vtiles, fit_count, width, width) if rows_dev == 8 else (vtiles, width, fit_count, width)
    flat = (slots_n * fit_count, width)
    whole, chosen = pl.pallas_call(
        functools.partial(comm_kernel, n, cap, fit_count),
        out_shape=(jax.ShapeDtypeStruct(v_shape, BF16), jax.ShapeDtypeStruct(flat, BF16)),
        in_specs=[smem, smem, vmem, vmem, vmem, vmem, vmem],
        out_specs=(vmem, vmem),
        scratch_shapes=[
            pltpu.VMEM((n, vtiles, rows_dev, 16, width), BF16),
            pltpu.VMEM(flat, BF16),
            pltpu.VMEM(flat, BF16),
            pltpu.VMEM(flat, BF16),
            dma((sends * CHUNKS,)),
            dma((n * CHUNKS,)),
            dma((n,)),
            dma((n,)),
            dma((n,)),
            dma((n,)),
        ],
        compiler_params=pltpu.CompilerParams(
            collective_id=0, has_side_effects=True, vmem_limit_bytes=48 * 2**20),
        name="gather_and_totals",
    )(perm, slot_fit, own, amplitudes, fits, code[:, None], code[None, :])
    if rows_dev != 8:
        whole = jnp.transpose(whole, (0, 2, 1, 3))
    chosen = chosen.reshape(slots_n, fit_count, width)
    flops = 4 * tiles_dev * fit_count * width**3
    return pl.pallas_call(
        ladder_kernel,
        out_shape=jax.ShapeDtypeStruct(amplitudes.shape, BF16),
        in_specs=[smem, smem, smem, smem, vmem, vmem, vmem, vmem],
        out_specs=vmem,
        compiler_params=pltpu.CompilerParams(vmem_limit_bytes=48 * 2**20),
        cost_estimate=pl.CostEstimate(flops=flops, bytes_accessed=12 * 2**20, transcendentals=0),
        name="ladder",
    )(tile_a, tile_b, fit_ids, slot, whole, amplitudes, fits, chosen)


def solution(mesh):
    in_specs = (
        P(("groups", "pairs"), None, None),
        P("groups", None),
        P("groups", "pairs", None, None),
        P(("groups", "pairs"), None, None, None),
    )
    out_specs = P(("groups", "pairs"), None, None)
    return jax.shard_map(body, mesh=mesh, in_specs=in_specs, out_specs=out_specs, check_vma=False)
```

```python
import functools

import jax
import jax.numpy as jnp
from jax import lax
from jax.experimental import pallas as pl
from jax.experimental.pallas import tpu as pltpu
from jax.sharding import PartitionSpec as P

F32 = jnp.float32
BF16 = jnp.bfloat16


CHUNKS = 4


def grid_of(n):
    ny = 2 if n == 16 else 1
    return n // (2 * ny), ny


def comm_kernel(
    n, cap, fit_count,
    perm_ref, row_ref, vv_ref, amp_ref, fit_ref, code_col_ref, code_row_ref,
    v_ref, chosen_ref,
    gbuf, part, inbuf, back,
    send_sem, recv_sem, go_send, go_recv, ret_send, ret_recv,
):
    nz, ny = grid_of(n)
    me = lax.axis_index("pairs")
    z, y, c = me // (2 * ny), (me // 2) % ny, me % 2
    vtiles, rows_dev = vv_ref.shape[0], vv_ref.shape[1]
    block = cap * fit_count

    def index(zz, yy, cc):
        return (zz * ny + yy) * 2 + cc

    barrier = pltpu.get_barrier_semaphore()
    for off in range(1, n):
        pl.semaphore_signal(barrier, inc=1, device_id={"pairs": (me + off) % n},
                            device_id_type=pl.DeviceIdType.MESH)
    pl.semaphore_wait(barrier, n - 1)

    def remote(src, dst, ssem, rsem, dev):
        return pltpu.make_async_remote_copy(
            src_ref=src, dst_ref=dst, send_sem=ssem, recv_sem=rsem,
            device_id={"pairs": dev}, device_id_type=pl.DeviceIdType.MESH)

    started = []

    per = vtiles // CHUNKS

    def send(src, shard, h, dev, cond):
        k = len(started)
        part_of = pl.ds(h * per, per)
        cp = remote(src.at[part_of], gbuf.at[shard, part_of], send_sem.at[k],
                    recv_sem.at[shard * CHUNKS + h], dev)
        started.append((cp, cond))
        if cond is None:
            cp.start()
        else:
            pl.when(cond)(cp.start)

    def arrived(shard, h, cond=None):
        ref = gbuf.at[shard, pl.ds(h * per, per)]
        cp = remote(ref, ref, send_sem.at[0], recv_sem.at[shard * CHUNKS + h], me)
        if cond is None:
            cp.wait_recv()
        else:
            pl.when(cond)(cp.wait_recv)

    up_ok, down_ok = z + 1 < nz, z >= 1
    up, down = jnp.minimum(z + 1, nz - 1), jnp.maximum(z - 1, 0)
    for h in range(CHUNKS):
        send(vv_ref, me, h, index(up, y, c), up_ok)
        send(vv_ref, me, h, index(down, y, c), down_ok)
        if ny == 2:
            send(vv_ref, me, h, index(z, 1 - y, c), None)
        send(vv_ref, me, h, index(z, y, 1 - c), None)

    def one_partial(s, carry):
        p = perm_ref[s]
        val = jnp.dot(fit_ref[row_ref[s]], amp_ref[p], preferred_element_type=F32)
        part[pl.ds(pl.multiple_of(s * fit_count, fit_count), fit_count), :] = val.astype(BF16)
        return carry

    lax.fori_loop(0, n * cap, one_partial, 0, unroll=4)

    def slab(ref, i):
        return ref.at[pl.ds(pl.multiple_of(i * block, block), block)]

    go = []
    for off in range(1, n):
        dev = (me + off) % n
        cp = remote(slab(part, dev), slab(inbuf, me), go_send.at[off], go_recv.at[off], dev)
        cp.start()
        go.append(cp)
    here = pl.ds(pl.multiple_of(me * block, block), block)
    inbuf[here, :] = part[here, :]

    def z_step(k):
        for h in range(CHUNKS):
            for zz, okay, nxt, nxt_ok in ((z - k, z >= k, up, up_ok), (z + k, z + k < nz, down, down_ok)):
                zs = jnp.clip(zz, 0, nz - 1)
                shard = index(zs, y, c)
                arrived(shard, h, okay)
                src = gbuf.at[shard]
                send(src, shard, h, index(nxt, y, c), jnp.logical_and(okay, nxt_ok))
                if ny == 2:
                    send(src, shard, h, index(z, 1 - y, c), okay)
                send(src, shard, h, index(z, y, 1 - c), okay)

    for k in range(1, nz):
        z_step(k)

    for cp in go:
        cp.wait_recv()
    total_rows = n * block
    mt = 256
    code_row = code_row_ref[...]
    values = inbuf[...]

    def totals(i, carry):
        r = pl.ds(pl.multiple_of(i * mt, mt), mt)
        same = jnp.where(code_col_ref[r, :] == code_row, 1.0, 0.0).astype(BF16)
        back[r, :] = jnp.dot(same, values, preferred_element_type=F32).astype(BF16)
        return carry

    lax.fori_loop(0, total_rows // mt, totals, 0)
    ret = []
    for off in range(1, n):
        dev = (me + off) % n
        cp = remote(slab(back, dev), slab(chosen_ref, me), ret_send.at[off], ret_recv.at[off], dev)
        cp.start()
        ret.append(cp)
    chosen_ref[here, :] = back[here, :]

    def relayout(lo, hi, m):
        if rows_dev != 8:
            return

        def one(i, carry):
            a0 = lo[i].astype(F32)
            a1 = hi[i].astype(F32)
            rows = pl.ds(pl.multiple_of(m * 16, 16), 16)
            for h in range(rows_dev):
                for e in range(2):
                    both = jnp.concatenate(
                        [a0[h, 8 * e:8 * e + 8], a1[h, 8 * e:8 * e + 8]], axis=0)
                    v_ref[i, 2 * h + e, rows, :] = both.astype(BF16)
            return carry

        lax.fori_loop(0, vtiles, one, 0)

    def chip(zz, yy):
        base = index(zz, yy, 0)
        relayout(gbuf.at[base], gbuf.at[base + 1], base // 2)

    gbuf[me] = vv_ref[...]
    for k in range(nz):
        zz = (z + k) % nz
        for h in range(CHUNKS):
            arrived(index(zz, y, 1 - c), h)
        chip(zz, y)
    if ny == 2:
        order = [(z, None)]
        for k in range(1, nz):
            order += [(z - k, z >= k), (z + k, z + k < nz)]
        for zz, cond in order:
            shard = index(jnp.clip(zz, 0, nz - 1), 1 - y, c)
            for h in range(CHUNKS):
                arrived(shard, h, cond)
                send(gbuf.at[shard], shard, h, index(z, y, 1 - c), cond)
        for zz, cond in order:
            zc = jnp.clip(zz, 0, nz - 1)

            def finish(zc=zc):
                for h in range(CHUNKS):
                    arrived(index(zc, 1 - y, 1 - c), h)
                chip(zc, 1 - y)

            if cond is None:
                finish()
            else:
                pl.when(cond)(finish)
    if rows_dev != 8:
        for i in range(n):
            v_ref[:, i * rows_dev:(i + 1) * rows_dev] = gbuf[i]
    for cp in ret:
        cp.wait_recv()
    for cp in go + ret:
        cp.wait_send()
    for cp, cond in started:
        if cond is None:
            cp.wait_send()
        else:
            pl.when(cond)(cp.wait_send)


def ladder_kernel(a_ids, b_ids, fit_ids, slots, v_ref, amp_ref, fit_ref, chosen_ref, out_ref):
    tiles = amp_ref.shape[0]
    q_count = v_ref.shape[1]
    width = v_ref.shape[2]

    def one(p, carry):
        left, right = v_ref[a_ids[p]], v_ref[b_ids[p]]
        wide = jnp.concatenate([right[q] for q in range(q_count)], axis=1)
        inner = jnp.dot(amp_ref[p], wide, preferred_element_type=F32).astype(BF16)
        tall = jnp.concatenate(
            [inner[:, q * width:(q + 1) * width] for q in range(q_count)], axis=0)
        acc = jnp.dot(
            jnp.concatenate([left[q] for q in range(q_count)], axis=1), tall,
            preferred_element_type=F32)
        cyc = lax.dot_general(
            fit_ref[fit_ids[p]], chosen_ref[slots[p]], (((0,), (0,)), ((), ())),
            preferred_element_type=F32).astype(BF16)
        out_ref[p] = (acc + cyc.astype(F32)).astype(BF16)
        return carry

    lax.fori_loop(0, tiles, one, 0, unroll=4)


def body(amplitudes, pair_tiles, fit_vv, fit_ov):
    tiles_dev, width = amplitudes.shape[0], amplitudes.shape[1]
    n = lax.axis_size("pairs")
    cap = max(2, tiles_dev // n)
    slots_n = n * cap
    occ_dev, vtiles, fit_count = fit_ov.shape[0], fit_ov.shape[1], fit_ov.shape[2]
    rows_dev = fit_vv.shape[1]
    here = lax.axis_index("pairs")
    mine = lax.dynamic_slice_in_dim(pair_tiles, here * tiles_dev, tiles_dev, 0)
    tile_a, tile_b = mine[:, 2], mine[:, 3]
    dest = mine[:, 1] // occ_dev
    fit_ids = mine[:, 0] % occ_dev * vtiles + tile_a
    steps = jnp.arange(tiles_dev, dtype=jnp.int32)
    earlier = steps[None, :] < steps[:, None]
    rank = jnp.sum(((dest[:, None] == dest[None, :]) & earlier).astype(jnp.int32), axis=1)
    slot = dest * cap + rank
    hit = (slot[None, :] == jnp.arange(slots_n, dtype=jnp.int32)[:, None]).astype(jnp.int32)
    perm = jnp.sum(hit * steps[None, :], axis=1)
    slot_fit = jnp.sum(hit * fit_ids[None, :], axis=1)

    every = pair_tiles.reshape(n, tiles_dev, 4)
    to_here = every[:, :, 1] // occ_dev == here
    order_in = jnp.sum((to_here[:, None, :] & earlier[None]).astype(jnp.int32), axis=2)
    column = every[:, :, 1] % occ_dev * vtiles + every[:, :, 3]
    picked = to_here[:, :, None] & (order_in[:, :, None] == jnp.arange(cap, dtype=jnp.int32))
    code = jnp.sum(jnp.where(picked, column[:, :, None] + 1, 0), axis=1) - 1
    code = code.reshape(slots_n, 1) * fit_count + jnp.arange(fit_count, dtype=jnp.int32)[None, :]
    code = code.reshape(slots_n * fit_count)

    own = fit_vv
    if rows_dev == 8:
        own = jnp.transpose(fit_vv, (0, 2, 1, 3)).reshape(vtiles, rows_dev, 16, width)
    fits = fit_ov.reshape(occ_dev * vtiles, fit_count, width)

    vmem = pl.BlockSpec(memory_space=pltpu.VMEM)
    smem = pl.BlockSpec(memory_space=pltpu.SMEM)
    nz, ny = grid_of(n)
    sends = 4 + 6 * (nz - 1) + 2 * nz
    dma = pltpu.SemaphoreType.DMA
    v_shape = (vtiles, fit_count, width, width) if rows_dev == 8 else (vtiles, width, fit_count, width)
    flat = (slots_n * fit_count, width)
    whole, chosen = pl.pallas_call(
        functools.partial(comm_kernel, n, cap, fit_count),
        out_shape=(jax.ShapeDtypeStruct(v_shape, BF16), jax.ShapeDtypeStruct(flat, BF16)),
        in_specs=[smem, smem, vmem, vmem, vmem, vmem, vmem],
        out_specs=(vmem, vmem),
        scratch_shapes=[
            pltpu.VMEM((n, vtiles, rows_dev, 16, width), BF16),
            pltpu.VMEM(flat, BF16),
            pltpu.VMEM(flat, BF16),
            pltpu.VMEM(flat, BF16),
            dma((sends * CHUNKS,)),
            dma((n * CHUNKS,)),
            dma((n,)),
            dma((n,)),
            dma((n,)),
            dma((n,)),
        ],
        compiler_params=pltpu.CompilerParams(
            collective_id=0, has_side_effects=True, vmem_limit_bytes=24 * 2**20),
        name="gather_and_totals",
    )(perm, slot_fit, own, amplitudes, fits, code[:, None], code[None, :])
    if rows_dev != 8:
        whole = jnp.transpose(whole, (0, 2, 1, 3))
    chosen = chosen.reshape(slots_n, fit_count, width)
    flops = 4 * tiles_dev * fit_count * width**3
    return pl.pallas_call(
        ladder_kernel,
        out_shape=jax.ShapeDtypeStruct(amplitudes.shape, BF16),
        in_specs=[smem, smem, smem, smem, vmem, vmem, vmem, vmem],
        out_specs=vmem,
        compiler_params=pltpu.CompilerParams(vmem_limit_bytes=24 * 2**20),
        cost_estimate=pl.CostEstimate(flops=flops, bytes_accessed=12 * 2**20, transcendentals=0),
        name="ladder",
    )(tile_a, tile_b, fit_ids, slot, whole, amplitudes, fits, chosen)


def solution(mesh):
    in_specs = (
        P(("groups", "pairs"), None, None),
        P("groups", None),
        P("groups", "pairs", None, None),
        P(("groups", "pairs"), None, None, None),
    )
    out_specs = P(("groups", "pairs"), None, None)
    return jax.shard_map(body, mesh=mesh, in_specs=in_specs, out_specs=out_specs, check_vma=False)
```

```python
import functools

import jax
import jax.numpy as jnp
from jax import lax
from jax.experimental import pallas as pl
from jax.experimental.pallas import tpu as pltpu
from jax.sharding import PartitionSpec as P

F32 = jnp.float32
BF16 = jnp.bfloat16


CHUNKS = 2


def grid_of(n):
    ny = 2 if n == 16 else 1
    return n // (2 * ny), ny


def comm_kernel(
    n, cap, fit_count,
    perm_ref, row_ref, vv_ref, amp_ref, fit_ref, code_col_ref, code_row_ref,
    v_ref, chosen_ref,
    gbuf, part, inbuf, back,
    send_sem, recv_sem, go_send, go_recv, ret_send, ret_recv,
):
    nz, ny = grid_of(n)
    me = lax.axis_index("pairs")
    z, y, c = me // (2 * ny), (me // 2) % ny, me % 2
    vtiles, rows_dev = vv_ref.shape[0], vv_ref.shape[1]
    block = cap * fit_count

    def index(zz, yy, cc):
        return (zz * ny + yy) * 2 + cc

    barrier = pltpu.get_barrier_semaphore()
    for off in range(1, n):
        pl.semaphore_signal(barrier, inc=1, device_id={"pairs": (me + off) % n},
                            device_id_type=pl.DeviceIdType.MESH)
    pl.semaphore_wait(barrier, n - 1)

    def remote(src, dst, ssem, rsem, dev):
        return pltpu.make_async_remote_copy(
            src_ref=src, dst_ref=dst, send_sem=ssem, recv_sem=rsem,
            device_id={"pairs": dev}, device_id_type=pl.DeviceIdType.MESH)

    started = []

    per = vtiles // CHUNKS

    def send(src, shard, h, dev, cond):
        k = len(started)
        part_of = pl.ds(h * per, per)
        cp = remote(src.at[part_of], gbuf.at[shard, part_of], send_sem.at[k],
                    recv_sem.at[shard * CHUNKS + h], dev)
        started.append((cp, cond))
        if cond is None:
            cp.start()
        else:
            pl.when(cond)(cp.start)

    def arrived(shard, h, cond=None):
        ref = gbuf.at[shard, pl.ds(h * per, per)]
        cp = remote(ref, ref, send_sem.at[0], recv_sem.at[shard * CHUNKS + h], me)
        if cond is None:
            cp.wait_recv()
        else:
            pl.when(cond)(cp.wait_recv)

    up_ok, down_ok = z + 1 < nz, z >= 1
    up, down = jnp.minimum(z + 1, nz - 1), jnp.maximum(z - 1, 0)
    for h in range(CHUNKS):
        send(vv_ref, me, h, index(up, y, c), up_ok)
        send(vv_ref, me, h, index(down, y, c), down_ok)
        if ny == 2:
            send(vv_ref, me, h, index(z, 1 - y, c), None)
        send(vv_ref, me, h, index(z, y, 1 - c), None)

    def one_partial(s, carry):
        p = perm_ref[s]
        val = jnp.dot(fit_ref[row_ref[s]], amp_ref[p], preferred_element_type=F32)
        part[pl.ds(pl.multiple_of(s * fit_count, fit_count), fit_count), :] = val.astype(BF16)
        return carry

    lax.fori_loop(0, n * cap, one_partial, 0, unroll=4)

    def slab(ref, i):
        return ref.at[pl.ds(pl.multiple_of(i * block, block), block)]

    go = []
    for off in range(1, n):
        dev = (me + off) % n
        cp = remote(slab(part, dev), slab(inbuf, me), go_send.at[off], go_recv.at[off], dev)
        cp.start()
        go.append(cp)
    here = pl.ds(pl.multiple_of(me * block, block), block)
    inbuf[here, :] = part[here, :]

    def z_step(k):
        for h in range(CHUNKS):
            for zz, okay, nxt, nxt_ok in ((z - k, z >= k, up, up_ok), (z + k, z + k < nz, down, down_ok)):
                zs = jnp.clip(zz, 0, nz - 1)
                shard = index(zs, y, c)
                arrived(shard, h, okay)
                src = gbuf.at[shard]
                send(src, shard, h, index(nxt, y, c), jnp.logical_and(okay, nxt_ok))
                if ny == 2:
                    send(src, shard, h, index(z, 1 - y, c), okay)
                send(src, shard, h, index(z, y, 1 - c), okay)

    for k in range(1, nz):
        z_step(k)

    for cp in go:
        cp.wait_recv()
    total_rows = n * block
    mt = 256
    code_row = code_row_ref[...]
    values = inbuf[...]

    def totals(i, carry):
        r = pl.ds(pl.multiple_of(i * mt, mt), mt)
        same = jnp.where(code_col_ref[r, :] == code_row, 1.0, 0.0).astype(BF16)
        back[r, :] = jnp.dot(same, values, preferred_element_type=F32).astype(BF16)
        return carry

    lax.fori_loop(0, total_rows // mt, totals, 0)
    ret = []
    for off in range(1, n):
        dev = (me + off) % n
        cp = remote(slab(back, dev), slab(chosen_ref, me), ret_send.at[off], ret_recv.at[off], dev)
        cp.start()
        ret.append(cp)
    chosen_ref[here, :] = back[here, :]

    def relayout(lo, hi, m):
        if rows_dev != 8:
            return

        def one(i, carry):
            a0 = lo[i].astype(F32)
            a1 = hi[i].astype(F32)
            rows = pl.ds(pl.multiple_of(m * 16, 16), 16)
            for h in range(rows_dev):
                for e in range(2):
                    both = jnp.concatenate(
                        [a0[h, 8 * e:8 * e + 8], a1[h, 8 * e:8 * e + 8]], axis=0)
                    v_ref[i, 2 * h + e, rows, :] = both.astype(BF16)
            return carry

        lax.fori_loop(0, vtiles, one, 0)

    def chip(zz, yy):
        base = index(zz, yy, 0)
        relayout(gbuf.at[base], gbuf.at[base + 1], base // 2)

    gbuf[me] = vv_ref[...]
    for k in range(nz):
        zz = (z + k) % nz
        for h in range(CHUNKS):
            arrived(index(zz, y, 1 - c), h)
        chip(zz, y)
    if ny == 2:
        order = [(z, None)]
        for k in range(1, nz):
            order += [(z - k, z >= k), (z + k, z + k < nz)]
        for zz, cond in order:
            shard = index(jnp.clip(zz, 0, nz - 1), 1 - y, c)
            for h in range(CHUNKS):
                arrived(shard, h, cond)
                send(gbuf.at[shard], shard, h, index(z, y, 1 - c), cond)
        for zz, cond in order:
            zc = jnp.clip(zz, 0, nz - 1)

            def finish(zc=zc):
                for h in range(CHUNKS):
                    arrived(index(zc, 1 - y, 1 - c), h)
                chip(zc, 1 - y)

            if cond is None:
                finish()
            else:
                pl.when(cond)(finish)
    if rows_dev != 8:
        for i in range(n):
            v_ref[:, i * rows_dev:(i + 1) * rows_dev] = gbuf[i]
    for cp in ret:
        cp.wait_recv()
    for cp in go + ret:
        cp.wait_send()
    for cp, cond in started:
        if cond is None:
            cp.wait_send()
        else:
            pl.when(cond)(cp.wait_send)


def ladder_kernel(a_ids, b_ids, fit_ids, slots, v_ref, amp_ref, fit_ref, chosen_ref, out_ref):
    tiles = amp_ref.shape[0]
    q_count = v_ref.shape[1]
    width = v_ref.shape[2]

    def one(p, carry):
        left, right = v_ref[a_ids[p]], v_ref[b_ids[p]]
        wide = jnp.concatenate([right[q] for q in range(q_count)], axis=1)
        inner = jnp.dot(amp_ref[p], wide, preferred_element_type=F32).astype(BF16)
        tall = jnp.concatenate(
            [inner[:, q * width:(q + 1) * width] for q in range(q_count)], axis=0)
        acc = jnp.dot(
            jnp.concatenate([left[q] for q in range(q_count)], axis=1), tall,
            preferred_element_type=F32)
        cyc = lax.dot_general(
            fit_ref[fit_ids[p]], chosen_ref[slots[p]], (((0,), (0,)), ((), ())),
            preferred_element_type=F32).astype(BF16)
        out_ref[p] = (acc + cyc.astype(F32)).astype(BF16)
        return carry

    lax.fori_loop(0, tiles, one, 0, unroll=8)


def body(amplitudes, pair_tiles, fit_vv, fit_ov):
    tiles_dev, width = amplitudes.shape[0], amplitudes.shape[1]
    n = lax.axis_size("pairs")
    cap = max(2, tiles_dev // n)
    slots_n = n * cap
    occ_dev, vtiles, fit_count = fit_ov.shape[0], fit_ov.shape[1], fit_ov.shape[2]
    rows_dev = fit_vv.shape[1]
    here = lax.axis_index("pairs")
    mine = lax.dynamic_slice_in_dim(pair_tiles, here * tiles_dev, tiles_dev, 0)
    tile_a, tile_b = mine[:, 2], mine[:, 3]
    dest = mine[:, 1] // occ_dev
    fit_ids = mine[:, 0] % occ_dev * vtiles + tile_a
    steps = jnp.arange(tiles_dev, dtype=jnp.int32)
    earlier = steps[None, :] < steps[:, None]
    rank = jnp.sum(((dest[:, None] == dest[None, :]) & earlier).astype(jnp.int32), axis=1)
    slot = dest * cap + rank
    hit = (slot[None, :] == jnp.arange(slots_n, dtype=jnp.int32)[:, None]).astype(jnp.int32)
    perm = jnp.sum(hit * steps[None, :], axis=1)
    slot_fit = jnp.sum(hit * fit_ids[None, :], axis=1)

    every = pair_tiles.reshape(n, tiles_dev, 4)
    to_here = every[:, :, 1] // occ_dev == here
    order_in = jnp.sum((to_here[:, None, :] & earlier[None]).astype(jnp.int32), axis=2)
    column = every[:, :, 1] % occ_dev * vtiles + every[:, :, 3]
    picked = to_here[:, :, None] & (order_in[:, :, None] == jnp.arange(cap, dtype=jnp.int32))
    code = jnp.sum(jnp.where(picked, column[:, :, None] + 1, 0), axis=1) - 1
    code = code.reshape(slots_n, 1) * fit_count + jnp.arange(fit_count, dtype=jnp.int32)[None, :]
    code = code.reshape(slots_n * fit_count)

    own = fit_vv
    if rows_dev == 8:
        own = jnp.transpose(fit_vv, (0, 2, 1, 3)).reshape(vtiles, rows_dev, 16, width)
    fits = fit_ov.reshape(occ_dev * vtiles, fit_count, width)

    vmem = pl.BlockSpec(memory_space=pltpu.VMEM)
    smem = pl.BlockSpec(memory_space=pltpu.SMEM)
    nz, ny = grid_of(n)
    sends = 4 + 6 * (nz - 1) + 2 * nz
    dma = pltpu.SemaphoreType.DMA
    v_shape = (vtiles, fit_count, width, width) if rows_dev == 8 else (vtiles, width, fit_count, width)
    flat = (slots_n * fit_count, width)
    whole, chosen = pl.pallas_call(
        functools.partial(comm_kernel, n, cap, fit_count),
        out_shape=(jax.ShapeDtypeStruct(v_shape, BF16), jax.ShapeDtypeStruct(flat, BF16)),
        in_specs=[smem, smem, vmem, vmem, vmem, vmem, vmem],
        out_specs=(vmem, vmem),
        scratch_shapes=[
            pltpu.VMEM((n, vtiles, rows_dev, 16, width), BF16),
            pltpu.VMEM(flat, BF16),
            pltpu.VMEM(flat, BF16),
            pltpu.VMEM(flat, BF16),
            dma((sends * CHUNKS,)),
            dma((n * CHUNKS,)),
            dma((n,)),
            dma((n,)),
            dma((n,)),
            dma((n,)),
        ],
        compiler_params=pltpu.CompilerParams(
            collective_id=0, has_side_effects=True, vmem_limit_bytes=24 * 2**20),
        name="gather_and_totals",
    )(perm, slot_fit, own, amplitudes, fits, code[:, None], code[None, :])
    if rows_dev != 8:
        whole = jnp.transpose(whole, (0, 2, 1, 3))
    chosen = chosen.reshape(slots_n, fit_count, width)
    flops = 4 * tiles_dev * fit_count * width**3
    return pl.pallas_call(
        ladder_kernel,
        out_shape=jax.ShapeDtypeStruct(amplitudes.shape, BF16),
        in_specs=[smem, smem, smem, smem, vmem, vmem, vmem, vmem],
        out_specs=vmem,
        compiler_params=pltpu.CompilerParams(vmem_limit_bytes=24 * 2**20),
        cost_estimate=pl.CostEstimate(flops=flops, bytes_accessed=12 * 2**20, transcendentals=0),
        name="ladder",
    )(tile_a, tile_b, fit_ids, slot, whole, amplitudes, fits, chosen)


def solution(mesh):
    in_specs = (
        P(("groups", "pairs"), None, None),
        P("groups", None),
        P("groups", "pairs", None, None),
        P(("groups", "pairs"), None, None, None),
    )
    out_specs = P(("groups", "pairs"), None, None)
    return jax.shard_map(body, mesh=mesh, in_specs=in_specs, out_specs=out_specs, check_vma=False)
```

```python
import functools

import jax
import jax.numpy as jnp
from jax import lax
from jax.experimental import pallas as pl
from jax.experimental.pallas import tpu as pltpu
from jax.sharding import PartitionSpec as P

F32 = jnp.float32
BF16 = jnp.bfloat16


CHUNKS = 2


def grid_of(n):
    ny = 2 if n == 16 else 1
    return n // (2 * ny), ny


def comm_kernel(
    n, cap, fit_count,
    perm_ref, row_ref, vv_ref, amp_ref, fit_ref, code_col_ref, code_row_ref,
    v_ref, chosen_ref,
    gbuf, part, inbuf, back,
    send_sem, recv_sem, go_send, go_recv, ret_send, ret_recv,
):
    nz, ny = grid_of(n)
    me = lax.axis_index("pairs")
    z, y, c = me // (2 * ny), (me // 2) % ny, me % 2
    vtiles, rows_dev = vv_ref.shape[0], vv_ref.shape[1]
    block = cap * fit_count

    def index(zz, yy, cc):
        return (zz * ny + yy) * 2 + cc

    barrier = pltpu.get_barrier_semaphore()
    for off in range(1, n):
        pl.semaphore_signal(barrier, inc=1, device_id={"pairs": (me + off) % n},
                            device_id_type=pl.DeviceIdType.MESH)
    pl.semaphore_wait(barrier, n - 1)

    def remote(src, dst, ssem, rsem, dev):
        return pltpu.make_async_remote_copy(
            src_ref=src, dst_ref=dst, send_sem=ssem, recv_sem=rsem,
            device_id={"pairs": dev}, device_id_type=pl.DeviceIdType.MESH)

    started = []

    per = vtiles // CHUNKS

    def send(src, shard, h, dev, cond):
        k = len(started)
        part_of = pl.ds(h * per, per)
        cp = remote(src.at[part_of], gbuf.at[shard, part_of], send_sem.at[k],
                    recv_sem.at[shard * CHUNKS + h], dev)
        started.append((cp, cond))
        if cond is None:
            cp.start()
        else:
            pl.when(cond)(cp.start)

    def arrived(shard, h, cond=None):
        ref = gbuf.at[shard, pl.ds(h * per, per)]
        cp = remote(ref, ref, send_sem.at[0], recv_sem.at[shard * CHUNKS + h], me)
        if cond is None:
            cp.wait_recv()
        else:
            pl.when(cond)(cp.wait_recv)

    up_ok, down_ok = z + 1 < nz, z >= 1
    up, down = jnp.minimum(z + 1, nz - 1), jnp.maximum(z - 1, 0)
    for h in range(CHUNKS):
        send(vv_ref, me, h, index(up, y, c), up_ok)
        send(vv_ref, me, h, index(down, y, c), down_ok)
        if ny == 2:
            send(vv_ref, me, h, index(z, 1 - y, c), None)
        send(vv_ref, me, h, index(z, y, 1 - c), None)

    def one_partial(s, carry):
        p = perm_ref[s]
        val = jnp.dot(fit_ref[row_ref[s]], amp_ref[p], preferred_element_type=F32)
        part[pl.ds(pl.multiple_of(s * fit_count, fit_count), fit_count), :] = val.astype(BF16)
        return carry

    lax.fori_loop(0, n * cap, one_partial, 0, unroll=4)

    def slab(ref, i):
        return ref.at[pl.ds(pl.multiple_of(i * block, block), block)]

    go = []
    for off in range(1, n):
        dev = (me + off) % n
        cp = remote(slab(part, dev), slab(inbuf, me), go_send.at[off], go_recv.at[off], dev)
        cp.start()
        go.append(cp)
    here = pl.ds(pl.multiple_of(me * block, block), block)
    inbuf[here, :] = part[here, :]

    def z_step(k):
        for h in range(CHUNKS):
            for zz, okay, nxt, nxt_ok in ((z - k, z >= k, up, up_ok), (z + k, z + k < nz, down, down_ok)):
                zs = jnp.clip(zz, 0, nz - 1)
                shard = index(zs, y, c)
                arrived(shard, h, okay)
                src = gbuf.at[shard]
                send(src, shard, h, index(nxt, y, c), jnp.logical_and(okay, nxt_ok))
                if ny == 2:
                    send(src, shard, h, index(z, 1 - y, c), okay)
                send(src, shard, h, index(z, y, 1 - c), okay)

    for k in range(1, nz):
        z_step(k)

    for cp in go:
        cp.wait_recv()
    total_rows = n * block
    mt = 256
    code_row = code_row_ref[...]
    values = inbuf[...]

    def totals(i, carry):
        r = pl.ds(pl.multiple_of(i * mt, mt), mt)
        same = jnp.where(code_col_ref[r, :] == code_row, 1.0, 0.0).astype(BF16)
        back[r, :] = jnp.dot(same, values, preferred_element_type=F32).astype(BF16)
        return carry

    lax.fori_loop(0, total_rows // mt, totals, 0)
    ret = []
    for off in range(1, n):
        dev = (me + off) % n
        cp = remote(slab(back, dev), slab(chosen_ref, me), ret_send.at[off], ret_recv.at[off], dev)
        cp.start()
        ret.append(cp)
    chosen_ref[here, :] = back[here, :]

    def relayout(lo, hi, m):
        if rows_dev != 8:
            return

        def one(i, carry):
            a0 = lo[i].astype(F32)
            a1 = hi[i].astype(F32)
            rows = pl.ds(pl.multiple_of(m * 16, 16), 16)
            for h in range(rows_dev):
                for e in range(2):
                    both = jnp.concatenate(
                        [a0[h, 8 * e:8 * e + 8], a1[h, 8 * e:8 * e + 8]], axis=0)
                    v_ref[i, 2 * h + e, rows, :] = both.astype(BF16)
            return carry

        lax.fori_loop(0, vtiles, one, 0)

    def chip(zz, yy):
        base = index(zz, yy, 0)
        relayout(gbuf.at[base], gbuf.at[base + 1], base // 2)

    gbuf[me] = vv_ref[...]
    for k in range(nz):
        zz = (z + k) % nz
        for h in range(CHUNKS):
            arrived(index(zz, y, 1 - c), h)
        chip(zz, y)
    if ny == 2:
        order = [(z, None)]
        for k in range(1, nz):
            order += [(z - k, z >= k), (z + k, z + k < nz)]
        for zz, cond in order:
            shard = index(jnp.clip(zz, 0, nz - 1), 1 - y, c)
            for h in range(CHUNKS):
                arrived(shard, h, cond)
                send(gbuf.at[shard], shard, h, index(z, y, 1 - c), cond)
        for zz, cond in order:
            zc = jnp.clip(zz, 0, nz - 1)

            def finish(zc=zc):
                for h in range(CHUNKS):
                    arrived(index(zc, 1 - y, 1 - c), h)
                chip(zc, 1 - y)

            if cond is None:
                finish()
            else:
                pl.when(cond)(finish)
    if rows_dev != 8:
        for i in range(n):
            v_ref[:, i * rows_dev:(i + 1) * rows_dev] = gbuf[i]
    for cp in ret:
        cp.wait_recv()
    for cp in go + ret:
        cp.wait_send()
    for cp, cond in started:
        if cond is None:
            cp.wait_send()
        else:
            pl.when(cond)(cp.wait_send)


def ladder_kernel(a_ids, b_ids, fit_ids, slots, v_ref, amp_ref, fit_ref, chosen_ref, out_ref):
    tiles = amp_ref.shape[0]
    q_count = v_ref.shape[1]
    width = v_ref.shape[2]

    def one(p, carry):
        left, right = v_ref[a_ids[p]], v_ref[b_ids[p]]
        wide = jnp.concatenate([right[q] for q in range(q_count)], axis=1)
        inner = jnp.dot(amp_ref[p], wide, preferred_element_type=F32).astype(BF16)
        tall = jnp.concatenate(
            [inner[:, q * width:(q + 1) * width] for q in range(q_count)], axis=0)
        acc = jnp.dot(
            jnp.concatenate([left[q] for q in range(q_count)], axis=1), tall,
            preferred_element_type=F32)
        cyc = lax.dot_general(
            fit_ref[fit_ids[p]], chosen_ref[slots[p]], (((0,), (0,)), ((), ())),
            preferred_element_type=F32).astype(BF16)
        out_ref[p] = (acc + cyc.astype(F32)).astype(BF16)
        return carry

    lax.fori_loop(0, tiles, one, 0, unroll=16)


def body(amplitudes, pair_tiles, fit_vv, fit_ov):
    tiles_dev, width = amplitudes.shape[0], amplitudes.shape[1]
    n = lax.axis_size("pairs")
    cap = max(2, tiles_dev // n)
    slots_n = n * cap
    occ_dev, vtiles, fit_count = fit_ov.shape[0], fit_ov.shape[1], fit_ov.shape[2]
    rows_dev = fit_vv.shape[1]
    here = lax.axis_index("pairs")
    mine = lax.dynamic_slice_in_dim(pair_tiles, here * tiles_dev, tiles_dev, 0)
    tile_a, tile_b = mine[:, 2], mine[:, 3]
    dest = mine[:, 1] // occ_dev
    fit_ids = mine[:, 0] % occ_dev * vtiles + tile_a
    steps = jnp.arange(tiles_dev, dtype=jnp.int32)
    earlier = steps[None, :] < steps[:, None]
    rank = jnp.sum(((dest[:, None] == dest[None, :]) & earlier).astype(jnp.int32), axis=1)
    slot = dest * cap + rank
    hit = (slot[None, :] == jnp.arange(slots_n, dtype=jnp.int32)[:, None]).astype(jnp.int32)
    perm = jnp.sum(hit * steps[None, :], axis=1)
    slot_fit = jnp.sum(hit * fit_ids[None, :], axis=1)

    every = pair_tiles.reshape(n, tiles_dev, 4)
    to_here = every[:, :, 1] // occ_dev == here
    order_in = jnp.sum((to_here[:, None, :] & earlier[None]).astype(jnp.int32), axis=2)
    column = every[:, :, 1] % occ_dev * vtiles + every[:, :, 3]
    picked = to_here[:, :, None] & (order_in[:, :, None] == jnp.arange(cap, dtype=jnp.int32))
    code = jnp.sum(jnp.where(picked, column[:, :, None] + 1, 0), axis=1) - 1
    code = code.reshape(slots_n, 1) * fit_count + jnp.arange(fit_count, dtype=jnp.int32)[None, :]
    code = code.reshape(slots_n * fit_count)

    own = fit_vv
    if rows_dev == 8:
        own = jnp.transpose(fit_vv, (0, 2, 1, 3)).reshape(vtiles, rows_dev, 16, width)
    fits = fit_ov.reshape(occ_dev * vtiles, fit_count, width)

    vmem = pl.BlockSpec(memory_space=pltpu.VMEM)
    smem = pl.BlockSpec(memory_space=pltpu.SMEM)
    nz, ny = grid_of(n)
    sends = 4 + 6 * (nz - 1) + 2 * nz
    dma = pltpu.SemaphoreType.DMA
    v_shape = (vtiles, fit_count, width, width) if rows_dev == 8 else (vtiles, width, fit_count, width)
    flat = (slots_n * fit_count, width)
    whole, chosen = pl.pallas_call(
        functools.partial(comm_kernel, n, cap, fit_count),
        out_shape=(jax.ShapeDtypeStruct(v_shape, BF16), jax.ShapeDtypeStruct(flat, BF16)),
        in_specs=[smem, smem, vmem, vmem, vmem, vmem, vmem],
        out_specs=(vmem, vmem),
        scratch_shapes=[
            pltpu.VMEM((n, vtiles, rows_dev, 16, width), BF16),
            pltpu.VMEM(flat, BF16),
            pltpu.VMEM(flat, BF16),
            pltpu.VMEM(flat, BF16),
            dma((sends * CHUNKS,)),
            dma((n * CHUNKS,)),
            dma((n,)),
            dma((n,)),
            dma((n,)),
            dma((n,)),
        ],
        compiler_params=pltpu.CompilerParams(
            collective_id=0, has_side_effects=True, vmem_limit_bytes=24 * 2**20),
        name="gather_and_totals",
    )(perm, slot_fit, own, amplitudes, fits, code[:, None], code[None, :])
    if rows_dev != 8:
        whole = jnp.transpose(whole, (0, 2, 1, 3))
    chosen = chosen.reshape(slots_n, fit_count, width)
    flops = 4 * tiles_dev * fit_count * width**3
    return pl.pallas_call(
        ladder_kernel,
        out_shape=jax.ShapeDtypeStruct(amplitudes.shape, BF16),
        in_specs=[smem, smem, smem, smem, vmem, vmem, vmem, vmem],
        out_specs=vmem,
        compiler_params=pltpu.CompilerParams(vmem_limit_bytes=24 * 2**20),
        cost_estimate=pl.CostEstimate(flops=flops, bytes_accessed=12 * 2**20, transcendentals=0),
        name="ladder",
    )(tile_a, tile_b, fit_ids, slot, whole, amplitudes, fits, chosen)


def solution(mesh):
    in_specs = (
        P(("groups", "pairs"), None, None),
        P("groups", None),
        P("groups", "pairs", None, None),
        P(("groups", "pairs"), None, None, None),
    )
    out_specs = P(("groups", "pairs"), None, None)
    return jax.shard_map(body, mesh=mesh, in_specs=in_specs, out_specs=out_specs, check_vma=False)
```
